256 devices in a mesh: dp: 32 (over x, z), seq: 8 (over y, core).
Axes of the slice: x: 4, y: 4, z: 8, core: 2. Of those that a mesh axis runs over, the one named last changes fastest.
Arguments:
- pixels: bfloat16 [32768, 1176], P(('dp', 'seq')), may hold values from -6 to 6
- patch_weight: bfloat16 [1176, 1280], replicated, may hold values from -0.1875 to 0.1875
- ln_gain: float32 [1280], replicated, may hold values from 0.1 to 1.9
- ln_bias: float32 [1280], replicated, may hold values from -1.5 to 1.5
- qkv_weight: bfloat16 [1280, 3840], P('dp'), may hold values from -4 to 4
- qkv_bias: float32 [3840], replicated, may hold values from -2.5 to 2.5
- out_weight: bfloat16 [1280, 1280], P('dp'), may hold values from -0.15625 to 0.15625
- out_bias: float32 [1280], replicated, may hold values from -1.5 to 1.5
- offsets: int32 [32, 3], P('dp'), may hold values from 0 to 854, as said below
- widths: int32 [32, 3], P('dp'), may hold values from 16 to 64
Outputs:
- encoded: bfloat16 [32768, 1280], P(('dp', 'seq'))
The draws below stay inside these ranges and needn't reach their ends.
Inputs may be any that keep to these rules, and one draw needn't show every extreme that they name: In every group the first offset is 0 and offsets rise; every image holds 170 or more tokens and the last image ends at position 1024; in some group the last image holds exactly 170 tokens.
All inputs are finite; a program needn't handle non-finite values.
Results may differ from the reference program's by a relative error of at most 0.012.
Values may be sent and summed in bfloat16 or wider, within the bound.
No kernel may reach another device: no remote copies, remote signals or barrier semaphores. Data moves between devices by JAX's collectives and lax.ppermute only.
A program may use at most 64 MiB of HBM per device.

```python
import jax
import jax.numpy as jnp
from jax import lax

D = 1280
HEADS = 16
HDIM = 80
PIX = 1176
IMGS = 3
WMIN = 16
WMAX = 64
GROUPS = 32
GROUP_TOK = 1024
TOKENS = 32768
SHARE = 4
MINLEN = 170
N_DP = 32
N_SEQ = 8


def draw_qkv_weight(key, part):
    normal_key = jax.random.fold_in(jax.random.fold_in(key, 5), 0)
    base = jnp.clip(jax.random.normal(normal_key, (D, 3 * D), jnp.float32), -3.0, 3.0) * D ** (-0.5)
    return base.astype(jnp.bfloat16)


def draw_offsets(key, part):
    cut_key, pick_key = jax.random.split(jax.random.fold_in(key, 11))
    slack = GROUP_TOK - IMGS * MINLEN
    cuts = jnp.sort(jax.random.randint(cut_key, (GROUPS, IMGS - 1), 0, slack + 1), axis=1)
    chosen = jax.random.randint(pick_key, (), 0, GROUPS)
    group_index = jnp.arange(GROUPS)[:, None]
    cuts = jnp.where(group_index == chosen, slack, cuts)
    edges = jnp.concatenate([jnp.zeros((GROUPS, 1), jnp.int32), cuts.astype(jnp.int32), jnp.full((GROUPS, 1), slack, jnp.int32)], axis=1)
    lengths = MINLEN + edges[:, 1:] - edges[:, :-1]
    starts = jnp.concatenate([jnp.zeros((GROUPS, 1), jnp.int32), jnp.cumsum(lengths, axis=1)[:, :-1]], axis=1)
    return starts.astype(jnp.int32)


def draw_widths(key, part):
    width_key, first_key, second_key = jax.random.split(jax.random.fold_in(key, 23), 3)
    total_slots = GROUPS * IMGS
    across = jax.random.randint(width_key, (total_slots,), WMIN, WMAX + 1)
    widest = jax.random.randint(first_key, (), 0, total_slots)
    narrowest = (widest + 1 + jax.random.randint(second_key, (), 0, total_slots - 1)) % total_slots
    slot_index = jnp.arange(total_slots)
    across = jnp.where(slot_index == widest, WMAX, across)
    across = jnp.where(slot_index == narrowest, WMIN, across)
    return across.reshape(GROUPS, IMGS).astype(jnp.int32)


def steps_of(own_key, shape, cuts, least, top_value):
    factor_of, own = 1.0, jax.random.fold_in(own_key, 6)
    for axis_at, blocks in cuts:
        heights = jnp.exp(jax.random.uniform(jax.random.fold_in(own, axis_at), (blocks,), jnp.float32, least / len(cuts), top_value / len(cuts)))
        factor_of = factor_of * jnp.repeat(heights, shape[axis_at] // blocks).reshape([-1 if axis == axis_at else 1 for axis in range(len(shape))])
    return factor_of


def centred(rng, extent, spread, limit, shards=(), held_as=jnp.bfloat16):
    drawn = spread * jax.random.normal(rng, extent, jnp.float32)
    if shards:
        drawn = drawn * steps_of(rng, extent, shards, -0.22, 0.18)
    return jnp.clip(drawn, -limit, limit).astype(held_as)


def setup_inputs(seed: int = 0) -> dict:
    splits = jax.random.split(jax.random.key(seed), 11)
    pixels = centred(splits[0], (TOKENS, PIX), 1.0, 6.0, ((0, 256),))
    patch_weight = centred(splits[1], (PIX, D), PIX ** -0.5, 0.1875)
    ln_gain = jnp.clip(1.0 + 0.18 * jax.random.normal(splits[2], (D,), jnp.float32), 0.1, 1.9)
    ln_bias = centred(splits[3], (D,), 0.3, 1.5, (), jnp.float32)
    qkv_weight = draw_qkv_weight(jax.random.fold_in(splits[10], 71), 0)
    qkv_bias = centred(splits[5], (3 * D,), 0.5, 2.5, (), jnp.float32)
    out_weight = centred(splits[6], (D, D), D ** -0.5, 0.15625, ((0, 32),))
    out_bias = centred(splits[7], (D,), 0.3, 1.5, (), jnp.float32)
    offsets = draw_offsets(jax.random.fold_in(splits[10], 71), 0)
    widths = draw_widths(jax.random.fold_in(splits[10], 71), 0)
    return dict(pixels=pixels, patch_weight=patch_weight, ln_gain=ln_gain, ln_bias=ln_bias, qkv_weight=qkv_weight, qkv_bias=qkv_bias, out_weight=out_weight, out_bias=out_bias, offsets=offsets, widths=widths)


def product(left, right):
    return jnp.dot(left.astype(jnp.float32), right.astype(jnp.float32), precision=lax.Precision.HIGHEST)

def image_lookup(positions, starts):
    return lax.optimization_barrier(jnp.sum((positions[:, None] >= starts[None, :]).astype(jnp.int32), axis=1)) - 1

def rotation_tables(positions, starts, image_widths, head_size):
    image_index = image_lookup(positions, starts)
    onehot = (image_index[:, None] == jnp.arange(starts.shape[0], dtype=jnp.int32)[None, :]).astype(jnp.int32)
    first_position = lax.optimization_barrier(jnp.sum(onehot * starts[None, :], axis=1))
    across = lax.optimization_barrier(jnp.sum(onehot * image_widths[None, :], axis=1))
    within = positions - first_position
    row_index = within // across
    column_index = within - row_index * across
    quarter = head_size // 4
    inverse = 1.0 / 10000.0 ** (jnp.arange(quarter, dtype=jnp.float32) * 2.0 / (head_size // 2))
    angles = jnp.concatenate([row_index.astype(jnp.float32)[:, None] * inverse[None, :], column_index.astype(jnp.float32)[:, None] * inverse[None, :]], axis=1)
    angles = jnp.concatenate([angles, angles], axis=1)
    return (jnp.cos(angles), jnp.sin(angles), image_index)

def rotate_heads(values, cosine, sine_table, head_size):
    half_size = head_size // 2
    turned = jnp.concatenate([-values[..., half_size:], values[..., :half_size]], axis=-1)
    return values * cosine[:, None, :] + turned * sine_table[:, None, :]

def layer_norm(embedded, ln_gain, ln_bias):
    values = embedded.astype(jnp.float32)
    center = values - lax.optimization_barrier(jnp.mean(values, axis=-1, keepdims=True))
    variance = lax.optimization_barrier(jnp.mean(center * center, axis=-1, keepdims=True))
    return (center * lax.rsqrt(variance + 1e-06) * ln_gain + ln_bias).astype(jnp.bfloat16)

def reference(pixels, patch_weight, ln_gain, ln_bias, qkv_weight, qkv_bias, out_weight, out_bias, offsets, widths):
    packed = pixels.reshape(N_DP, N_SEQ, N_DP, SHARE, PIX).transpose(2, 1, 0, 3, 4).reshape(N_DP, GROUP_TOK, PIX)
    score_scale = HDIM ** (-0.5)

    def one_group(inputs):
        group_pixels, starts, image_widths = inputs
        embedded = product(group_pixels, patch_weight).astype(jnp.bfloat16)
        normed = layer_norm(embedded, ln_gain, ln_bias)
        projected = product(normed, qkv_weight) + qkv_bias
        positions = jnp.arange(GROUP_TOK, dtype=jnp.int32)
        cosine, sine_table, image_index = rotation_tables(positions, starts, image_widths, HDIM)
        queries = rotate_heads(projected[:, :D].reshape(GROUP_TOK, HEADS, HDIM), cosine, sine_table, HDIM).astype(jnp.bfloat16)
        key_rows = rotate_heads(projected[:, D:2 * D].reshape(GROUP_TOK, HEADS, HDIM), cosine, sine_table, HDIM).astype(jnp.bfloat16)
        values = projected[:, 2 * D:].reshape(GROUP_TOK, HEADS, HDIM).astype(jnp.bfloat16)
        allowed = image_index[:, None] == image_index[None, :]

        def one_head(triple):
            head_queries, head_keys, head_values = triple
            scores = product(head_queries, head_keys.T) * score_scale
            largest = lax.optimization_barrier(jnp.max(jnp.where(allowed, scores, -jnp.inf), axis=1))
            weights = jnp.where(allowed, jnp.exp(scores - largest[:, None]), 0.0)
            denominator = lax.optimization_barrier(jnp.sum(weights, axis=1))
            numerator = product(weights.astype(jnp.bfloat16), head_values)
            return numerator / denominator[:, None]
        attended = lax.map(one_head, (queries.transpose(1, 0, 2), key_rows.transpose(1, 0, 2), values.transpose(1, 0, 2)))
        attended = attended.transpose(1, 0, 2).reshape(GROUP_TOK, D).astype(jnp.bfloat16)
        return (embedded.astype(jnp.float32) + product(attended, out_weight) + out_bias).astype(jnp.bfloat16)
    encoded = lax.map(one_group, (packed, offsets, widths))
    return encoded.reshape(TOKENS, D)
```

```python
import functools

import jax
import jax.numpy as jnp
import numpy as np
from jax import lax
from jax.experimental import pallas as pl
from jax.experimental.pallas import tpu as pltpu
from jax.sharding import PartitionSpec as P

HEADS = 16
HDIM = 80
D = 1280
OWN = 2 * HDIM
WIDE = 768
VMEM_LIMIT = 56 * 1024 * 1024
BF16, F32 = jnp.bfloat16, jnp.float32

VM = pl.BlockSpec(memory_space=pltpu.VMEM)
SM = pl.BlockSpec(memory_space=pltpu.SMEM)


def params():
    return pltpu.CompilerParams(vmem_limit_bytes=VMEM_LIMIT)


def seq_shift(dy):
    return [((i + 2 * dy) % 8, i) for i in range(8)]


SWAP = [(i, i ^ 1) for i in range(8)]


def dp_shift(dx, dz):
    return [
        (((x + dx) % 4) * 8 + (z + dz) % 8, x * 8 + z) for x in range(4) for z in range(8)
    ]


def from_seq(value, dy):
    return lax.ppermute(value, "seq", seq_shift(dy))


def swap(value):
    return lax.ppermute(value, "seq", SWAP)


def from_dp(value, dx, dz):
    return lax.ppermute(value, "dp", dp_shift(dx, dz))


def embed_kernel(px, pw, gain, bias, emb_out, norm_out):
    emb = jnp.dot(px[...], pw[...], preferred_element_type=F32).astype(BF16)
    emb_out[...] = emb
    v = emb.astype(F32)
    center = v - jnp.mean(v, axis=-1, keepdims=True)
    var = jnp.mean(center * center, axis=-1, keepdims=True)
    norm_out[...] = (center * lax.rsqrt(var + 1e-06) * gain[...] + bias[...]).astype(BF16)


def lay_kernel(place, *refs):
    blocks, out = refs[:8], refs[8]
    col = lax.broadcasted_iota(jnp.int32, (3 * OWN, WIDE), 0)
    lane = lax.broadcasted_iota(jnp.int32, (3 * OWN, WIDE), 1)
    piece = sum((col >= HDIM * k).astype(jnp.int32) for k in range(1, 5))
    high = ((col - HDIM * piece >= HDIM // 2) & (col < 4 * HDIM)).astype(jnp.int32)
    pick = (lane == col + 48 * piece + 24 * high).astype(F32).astype(BF16)
    x, z = place[0], place[1]
    for dz in range(8):
        wide = jnp.dot(blocks[dz][...], pick, preferred_element_type=F32).astype(BF16)
        for dx in range(4):
            at = lax.rem(x + dx, 4) * 8 + lax.rem(z + dz, 8)
            out[at] = wide[dx * 40 : dx * 40 + 40]


def out_lay_kernel(place, *refs):
    out = refs[8]
    x, z, c = place[0], place[1], place[2]
    for half in range(2):
        first = pl.multiple_of(jnp.bitwise_xor(c, half) * 640, 128)
        for dx in range(4):
            for dz in range(8):
                at = lax.rem(x + dx, 4) * 8 + lax.rem(z + dz, 8)
                out[at, :, pl.ds(first, 640)] = refs[half * 4 + dx][dz]


def attend_kernel(place, *refs):
    shards = refs[:8]
    w, b, cosine, sine = refs[8:12]
    own_out, other_out = refs[12:14]
    qs, ks, vs = refs[14:17]
    scale = float(HDIM**-0.5 * np.log2(np.e))
    y, c, o1, o2 = place[0], place[1], place[2], place[3]

    def first_of(r):
        return (lax.rem(y + r // 2, 4) * 2 + jnp.bitwise_xor(c, r % 2)) * 128

    def image(p):
        return (p >= o1).astype(jnp.int32) + (p >= o2).astype(jnp.int32)

    for blk in range(4):
        rows = pl.ds(blk * 256, 256)
        x = jnp.concatenate([shards[2 * blk][...], shards[2 * blk + 1][...]], axis=0)
        proj = jnp.dot(x, w[...], preferred_element_type=F32) + b[...]
        cs, sn = cosine[rows, :], sine[rows, :]
        for h in range(2):
            for first, dst in ((0, qs), (256, ks)):
                t = proj[:, first + h * 128 : first + h * 128 + 128]
                dst[h, rows, :] = (t * cs + pltpu.roll(t, 64, 1) * sn).astype(BF16)
        vs[rows, :] = proj[:, 512:].astype(BF16)
    lane = lax.broadcasted_iota(jnp.int32, (1, 128), 1)
    key_image = jnp.concatenate([image(lane + first_of(r)) for r in range(8)], axis=1)
    row = lax.broadcasted_iota(jnp.int32, (128, 1), 0)
    wide_lane = lax.broadcasted_iota(jnp.int32, (256, 256), 1)
    for blk in range(4):
        rows = pl.ds(blk * 256, 256)
        query_image = jnp.concatenate(
            [image(row + first_of(2 * blk)), image(row + first_of(2 * blk + 1))], axis=0
        )
        allowed = query_image == key_image
        done = []
        for h in range(2):
            s = lax.dot_general(
                qs[h, rows, :], ks[h], (((1,), (1,)), ((), ())), preferred_element_type=F32
            )
            s = jnp.where(allowed, s, -1e30)
            m = jnp.max(s, axis=1, keepdims=True)
            p = jnp.exp2((s - m) * scale).astype(BF16)
            o = jnp.dot(p, vs[...], preferred_element_type=F32)
            done.append(o / o[:, OWN : OWN + 1])
        att = jnp.where(wide_lane < HDIM, done[0], done[1])[:, :OWN].astype(BF16)
        own_out[blk] = att[:128]
        other_out[blk] = att[128:]


def out_kernel(place, a0, a1, a2, a3, w, emb, bias, out):
    y, c = place[0], place[1]
    acc = emb[...].astype(F32) + bias[...]
    for dy, a in enumerate((a0, a1, a2, a3)):
        for dc in range(2):
            s = lax.rem(y + dy, 4) * 2 + jnp.bitwise_xor(c, dc)
            acc += jnp.dot(a[dc], w[s], preferred_element_type=F32)
    out[...] = acc.astype(BF16)


def halves_apart(piece):
    zero = jnp.zeros(piece.shape[:-1] + (24,), piece.dtype)
    return jnp.concatenate([piece[..., :40], zero, piece[..., 40:], zero], axis=-1)


INVERSE = np.zeros((1, 128), np.float32)
for _l in range(128):
    if _l % 64 < 40:
        INVERSE[0, _l] = 1.0 / 10000.0 ** ((_l % 64 % 20) * 2.0 / 40.0)


def rotation_tables(y, c, starts, widths):
    token = lax.broadcasted_iota(jnp.int32, (1024, 128), 0)
    lane = lax.broadcasted_iota(jnp.int32, (1024, 128), 1)
    r = token // 128
    pos = ((y + r // 2) % 4 * 2 + (c ^ (r % 2))) * 128 + token % 128
    second, third = pos >= starts[1], pos >= starts[2]
    first = jnp.where(third, starts[2], jnp.where(second, starts[1], starts[0]))
    across = jnp.where(third, widths[2], jnp.where(second, widths[1], widths[0]))
    within = pos - first
    row = within // across
    column = within - row * across
    low = lane % 64
    angle = jnp.where(low < 20, row, column).astype(F32) * INVERSE
    sign = jnp.where(lane < 64, -1.0, 1.0)
    return jnp.cos(angle), jnp.sin(angle) * sign


def per_device(
    pixels,
    patch_weight,
    ln_gain,
    ln_bias,
    qkv_weight,
    qkv_bias,
    out_weight,
    out_bias,
    offsets,
    widths,
):
    dp, seq = lax.axis_index("dp"), lax.axis_index("seq")
    x, z, y, c = dp // 8, dp % 8, seq // 2, seq % 2
    rows = jax.ShapeDtypeStruct((128, D), BF16)

    local_pixels = lax.all_to_all(pixels, "dp", split_axis=0, concat_axis=0, tiled=True)

    mine = jnp.concatenate(
        [lax.dynamic_slice_in_dim(qkv_weight, k * D + seq * OWN, OWN, 1) for k in range(3)], axis=1
    )
    xs = [mine] + [from_dp(mine, d, 0) for d in (1, 2, 3)]
    z0 = jnp.concatenate(xs, axis=0)
    z1, z7 = from_dp(z0, 0, 1), from_dp(z0, 0, 7)
    z2, z6 = from_dp(z1, 0, 1), from_dp(z7, 0, 7)
    z3, z5 = from_dp(z2, 0, 1), from_dp(z6, 0, 7)
    z4 = from_dp(z3, 0, 1)
    place_dp = jnp.stack([x, z, c]).astype(jnp.int32)
    laid = pl.pallas_call(
        lay_kernel,
        out_shape=jax.ShapeDtypeStruct((32, 40, WIDE), BF16),
        in_specs=[SM] + [VM] * 8,
        out_specs=VM,
        compiler_params=params(),
        name="lay_qkv",
    )(place_dp, z0, z1, z2, z3, z4, z5, z6, z7).reshape(D, WIDE)

    own_bias = [lax.dynamic_slice_in_dim(qkv_bias, k * D + seq * OWN, OWN, 0) for k in range(3)]
    ones = jnp.ones((1,), F32)
    laid_bias = jnp.concatenate(
        [halves_apart(own_bias[k][h * HDIM : (h + 1) * HDIM]) for k in range(2) for h in range(2)]
        + [own_bias[2], ones, jnp.zeros((95,), F32)]
    )[None]

    half = lax.dynamic_slice_in_dim(out_weight, c * 640, 640, 1)[None]
    h1, h7 = from_dp(half, 0, 1), from_dp(half, 0, 7)
    h234 = from_dp(jnp.concatenate([h7, half, h1]), 0, 3)
    h56 = from_dp(jnp.concatenate([half, h1]), 0, 5)
    column0 = jnp.concatenate([half, h1, h234, h56, h7])
    columns = [column0] + [from_dp(column0, d, 0) for d in (1, 2, 3)]
    others = [swap(v) for v in columns]
    out_laid = pl.pallas_call(
        out_lay_kernel,
        out_shape=jax.ShapeDtypeStruct((32, 40, D), BF16),
        in_specs=[SM] + [VM] * 8,
        out_specs=VM,
        compiler_params=params(),
        name="lay_out",
    )(place_dp, *columns, *others).reshape(8, OWN, D)

    embedded, normed = pl.pallas_call(
        embed_kernel,
        out_shape=(rows, rows),
        in_specs=[VM] * 4,
        out_specs=(VM, VM),
        compiler_params=params(),
        name="embed",
    )(local_pixels, patch_weight, ln_gain[None], ln_bias[None])

    same = [normed] + [from_seq(normed, d) for d in (1, 2, 3)]
    crossed = [swap(v) for v in same]
    shards = [v for pair in zip(same, crossed) for v in pair]

    starts, across = offsets[0], widths[0]
    cosine, sine = rotation_tables(y, c, starts, across)
    place = jnp.stack([y, c, starts[1], starts[2]]).astype(jnp.int32)
    part = jax.ShapeDtypeStruct((4, 128, OWN), BF16)
    own_tokens, other_tokens = pl.pallas_call(
        attend_kernel,
        out_shape=(part, part),
        in_specs=[SM] + [VM] * 12,
        out_specs=(VM, VM),
        scratch_shapes=[
            pltpu.VMEM((2, 1024, 128), BF16),
            pltpu.VMEM((2, 1024, 128), BF16),
            pltpu.VMEM((1024, 256), BF16),
        ],
        compiler_params=params(),
        name="attend",
    )(place, *shards, laid, laid_bias, cosine, sine)

    from_core = swap(other_tokens)
    pairs = [jnp.stack([own_tokens[d], from_core[d]]) for d in range(4)]
    got = [pairs[0]] + [from_seq(pairs[(4 - d) % 4], d) for d in (1, 2, 3)]
    return pl.pallas_call(
        out_kernel,
        out_shape=rows,
        in_specs=[SM] + [VM] * 7,
        out_specs=VM,
        compiler_params=params(),
        name="project",
    )(jnp.stack([y, c]).astype(jnp.int32), *got, out_laid, embedded, out_bias[None])


def solution(mesh):
    in_specs = (
        P(("dp", "seq"), None),
        P(),
        P(),
        P(),
        P("dp", None),
        P(),
        P("dp", None),
        P(),
        P("dp", None),
        P("dp", None),
    )
    out_specs = P(("dp", "seq"), None)
    return jax.shard_map(
        per_device, mesh=mesh, in_specs=in_specs, out_specs=out_specs, check_vma=False
    )
```

```python
import functools

import jax
import jax.numpy as jnp
import numpy as np
from jax import lax
from jax.experimental import pallas as pl
from jax.experimental.pallas import tpu as pltpu
from jax.sharding import PartitionSpec as P

HEADS = 16
HDIM = 80
D = 1280
OWN = 2 * HDIM
WIDE = 768
BF16, F32 = jnp.bfloat16, jnp.float32

VM = pl.BlockSpec(memory_space=pltpu.VMEM)
SM = pl.BlockSpec(memory_space=pltpu.SMEM)


def params(mib):
    return pltpu.CompilerParams(vmem_limit_bytes=mib * 1024 * 1024)


def after(value, *earlier):
    return lax.optimization_barrier((value, *earlier))[0]


def seq_shift(dy):
    return [((i + 2 * dy) % 8, i) for i in range(8)]


SWAP = [(i, i ^ 1) for i in range(8)]


def dp_shift(dx, dz):
    return [
        (((x + dx) % 4) * 8 + (z + dz) % 8, x * 8 + z) for x in range(4) for z in range(8)
    ]


def from_seq(value, dy):
    return lax.ppermute(value, "seq", seq_shift(dy))


def swap(value):
    return lax.ppermute(value, "seq", SWAP)


def from_dp(value, dx, dz):
    return lax.ppermute(value, "dp", dp_shift(dx, dz))


def embed_kernel(px, pw, gain, bias, emb_out, norm_out):
    emb = jnp.dot(px[...], pw[...], preferred_element_type=F32).astype(BF16)
    emb_out[...] = emb
    v = emb.astype(F32)
    center = v - jnp.mean(v, axis=-1, keepdims=True)
    var = jnp.mean(center * center, axis=-1, keepdims=True)
    scaled = center * lax.rsqrt(var + 1e-06) * gain[...][None]
    norm_out[...] = (scaled + bias[...][None]).astype(BF16)


def lay_kernel(place, *refs):
    blocks, out = refs[:8], refs[8]
    col = lax.broadcasted_iota(jnp.int32, (3 * OWN, WIDE), 0)
    lane = lax.broadcasted_iota(jnp.int32, (3 * OWN, WIDE), 1)
    piece = sum((col >= HDIM * k).astype(jnp.int32) for k in range(1, 5))
    high = ((col - HDIM * piece >= HDIM // 2) & (col < 4 * HDIM)).astype(jnp.int32)
    pick = (lane == col + 48 * piece + 24 * high).astype(F32).astype(BF16)
    x, z = place[0], place[1]
    for dz in range(8):
        wide = jnp.dot(blocks[dz][...], pick, preferred_element_type=F32).astype(BF16)
        for dx in range(4):
            at = lax.rem(x + dx, 4) * 8 + lax.rem(z + dz, 8)
            out[at] = wide[dx * 40 : dx * 40 + 40]


def out_lay_kernel(place, *refs):
    out = refs[8]
    x, z, c = place[0], place[1], place[3]
    for half in range(2):
        first = pl.multiple_of(jnp.bitwise_xor(c, half) * 640, 128)
        for dx in range(4):
            for dz in range(8):
                at = lax.rem(x + dx, 4) * 8 + lax.rem(z + dz, 8)
                out[at, :, pl.ds(first, 640)] = refs[half * 4 + dx][dz]


def tables_kernel(place, inverse, cos_out, sin_out):
    y, c = place[2], place[3]
    o0, o1, o2 = place[4], place[5], place[6]
    lane = lax.broadcasted_iota(jnp.int32, (128, 128), 1)
    sub = lax.broadcasted_iota(jnp.int32, (128, 128), 0)
    low = jnp.bitwise_and(lane, 63)
    angle = jnp.bitwise_and(sub, 63).astype(F32) * inverse[...]
    mine = (low < HDIM // 4) == (sub < 64)
    both = jnp.concatenate(
        [
            jnp.where(mine, jnp.cos(angle), 0.0),
            jnp.where(mine, jnp.sin(angle) * jnp.where(lane < 64, -1.0, 1.0), 0.0),
        ],
        axis=1,
    )
    parts = []
    for _ in range(3):
        parts.append(both.astype(BF16))
        both = both - parts[-1].astype(F32)
    for r in range(8):
        first = (lax.rem(y + r // 2, 4) * 2 + jnp.bitwise_xor(c, r % 2)) * 128
        pos = first + sub
        second, third = pos >= o1, pos >= o2
        start = jnp.where(third, o2, jnp.where(second, o1, o0))
        across = jnp.where(third, place[9], jnp.where(second, place[8], place[7]))
        within = pos - start
        row = ((within.astype(F32) + 0.5) / across.astype(F32)).astype(jnp.int32)
        column = within - row * across
        pick = (jnp.where(lane < 64, row, column + 64) == lane).astype(F32).astype(BF16)
        total = sum(jnp.dot(pick, part, preferred_element_type=F32) for part in parts)
        cos_out[r] = total[:, :128]
        sin_out[r] = total[:, 128:]


def attend_kernel(place, *refs):
    shards = refs[:8]
    w, b, cosine, sine = refs[8:12]
    outs = refs[12:16]
    qs, ks, vs = refs[16:19]
    scale = float(HDIM**-0.5 * np.log2(np.e))
    y, c, o1, o2 = place[2], place[3], place[5], place[6]

    def first_of(r):
        return (lax.rem(y + r // 2, 4) * 2 + jnp.bitwise_xor(c, r % 2)) * 128

    def image(p):
        return (p >= o1).astype(jnp.int32) + (p >= o2).astype(jnp.int32)

    for blk in range(4):
        rows = pl.ds(blk * 256, 256)
        x = jnp.concatenate([shards[2 * blk][...], shards[2 * blk + 1][...]], axis=0)
        proj = jnp.dot(x, w[...], preferred_element_type=F32) + b[...][None]
        cs = cosine[2 * blk : 2 * blk + 2].reshape(256, 128)
        sn = sine[2 * blk : 2 * blk + 2].reshape(256, 128)
        for h in range(2):
            for first, dst in ((0, qs), (256, ks)):
                t = proj[:, first + h * 128 : first + h * 128 + 128]
                dst[h, rows, :] = (t * cs + pltpu.roll(t, 64, 1) * sn).astype(BF16)
        vs[rows, :] = proj[:, 512:].astype(BF16)
    lane = lax.broadcasted_iota(jnp.int32, (1, 128), 1)
    key_image = jnp.concatenate([image(lane + first_of(r)) for r in range(8)], axis=1)
    row = lax.broadcasted_iota(jnp.int32, (128, 1), 0)
    wide_lane = lax.broadcasted_iota(jnp.int32, (256, 256), 1)
    for blk in range(4):
        rows = pl.ds(blk * 256, 256)
        query_image = jnp.concatenate(
            [image(row + first_of(2 * blk)), image(row + first_of(2 * blk + 1))], axis=0
        )
        allowed = query_image == key_image
        done = []
        for h in range(2):
            s = lax.dot_general(
                qs[h, rows, :], ks[h], (((1,), (1,)), ((), ())), preferred_element_type=F32
            )
            s = jnp.where(allowed, s, -1e30)
            m = jnp.max(s, axis=1, keepdims=True)
            p = jnp.exp2((s - m) * scale).astype(BF16)
            o = jnp.dot(p, vs[...], preferred_element_type=F32)
            done.append(o / o[:, OWN : OWN + 1])
        att = jnp.where(wide_lane < HDIM, done[0], done[1])[:, :OWN]
        outs[blk][...] = jnp.concatenate([att[:128], att[128:]], axis=1).astype(BF16)


def out_kernel(place, *refs):
    here, there = refs[:4], refs[4:8]
    w, emb, bias, out = refs[8:]
    y, c = place[2], place[3]
    acc = emb[...].astype(F32) + bias[...][None]
    for dy in range(4):
        chip = lax.rem(y + dy, 4) * 2
        acc += jnp.dot(here[dy][:, :OWN], w[chip + c], preferred_element_type=F32)
        acc += jnp.dot(there[dy][:, OWN:], w[chip + 1 - c], preferred_element_type=F32)
    out[...] = acc.astype(BF16)


def halves_apart(piece):
    zero = jnp.zeros(piece.shape[:-1] + (24,), piece.dtype)
    return jnp.concatenate([piece[..., :40], zero, piece[..., 40:], zero], axis=-1)


INVERSE = np.zeros((1, 128), np.float32)
for _l in range(128):
    if _l % 64 < 40:
        INVERSE[0, _l] = 1.0 / 10000.0 ** ((_l % 64 % 20) * 2.0 / 40.0)


def per_device(
    pixels,
    patch_weight,
    ln_gain,
    ln_bias,
    qkv_weight,
    qkv_bias,
    out_weight,
    out_bias,
    offsets,
    widths,
):
    dp, seq = lax.axis_index("dp"), lax.axis_index("seq")
    x, z, y, c = dp // 8, dp % 8, seq // 2, seq % 2
    rows = jax.ShapeDtypeStruct((128, D), BF16)
    place = jnp.concatenate(
        [jnp.stack([x, z, y, c]).astype(jnp.int32), offsets[0], widths[0], jnp.zeros((6,), jnp.int32)]
    )

    blocks = pixels.reshape(32, 4, -1)
    local_pixels = lax.all_to_all(blocks, "dp", 0, 0, tiled=True).reshape(128, -1)

    slices = [lax.dynamic_slice_in_dim(qkv_weight, k * D + seq * OWN, OWN, 1) for k in range(3)]
    mine = after(jnp.concatenate(slices, axis=1), blocks)
    xs = [mine] + [from_dp(mine, d, 0) for d in (1, 2, 3)]
    z0 = jnp.concatenate(xs, axis=0)
    z1, z7 = from_dp(z0, 0, 1), from_dp(z0, 0, 7)
    z2, z6 = from_dp(z1, 0, 1), from_dp(z7, 0, 7)

    half = after(lax.dynamic_slice_in_dim(out_weight, c * 640, 640, 1)[None], z0)
    h1, h7 = from_dp(half, 0, 1), from_dp(half, 0, 7)

    cosine, sine = pl.pallas_call(
        tables_kernel,
        out_shape=(jax.ShapeDtypeStruct((8, 128, 128), F32),) * 2,
        in_specs=[SM, VM],
        out_specs=(VM, VM),
        compiler_params=params(6),
        name="tables",
    )(place, jnp.asarray(INVERSE))

    embedded, normed = pl.pallas_call(
        embed_kernel,
        out_shape=(rows, rows),
        in_specs=[VM] * 4,
        out_specs=(VM, VM),
        compiler_params=params(12),
        name="embed",
    )(local_pixels, patch_weight, ln_gain, ln_bias)

    same = [normed] + [from_seq(normed, d) for d in (1, 2, 3)]
    crossed = [swap(v) for v in same]
    shards = [v for pair in zip(same, crossed) for v in pair]

    z2, z6 = after(z2, normed), after(z6, normed)
    z3, z5 = from_dp(z2, 0, 1), from_dp(z6, 0, 7)
    z4 = from_dp(z3, 0, 1)
    laid = pl.pallas_call(
        lay_kernel,
        out_shape=jax.ShapeDtypeStruct((32, 40, WIDE), BF16),
        in_specs=[SM] + [VM] * 8,
        out_specs=VM,
        compiler_params=params(12),
        name="lay_qkv",
    )(place, z0, z1, z2, z3, z4, z5, z6, z7).reshape(D, WIDE)

    own_bias = [lax.dynamic_slice_in_dim(qkv_bias, k * D + seq * OWN, OWN, 0) for k in range(3)]
    ones = jnp.ones((1,), F32)
    laid_bias = jnp.concatenate(
        [halves_apart(own_bias[k][h * HDIM : (h + 1) * HDIM]) for k in range(2) for h in range(2)]
        + [own_bias[2], ones, jnp.zeros((95,), F32)]
    )

    half, h1, h7 = (after(v, normed) for v in (half, h1, h7))
    h234 = from_dp(jnp.concatenate([h7, half, h1]), 0, 3)
    h56 = from_dp(jnp.concatenate([half, h1]), 0, 5)
    column0 = jnp.concatenate([half, h1, h234, h56, h7])
    columns = [column0] + [from_dp(column0, d, 0) for d in (1, 2, 3)]

    parts = pl.pallas_call(
        attend_kernel,
        out_shape=(jax.ShapeDtypeStruct((128, 2 * OWN), BF16),) * 4,
        in_specs=[SM] + [VM] * 12,
        out_specs=(VM,) * 4,
        scratch_shapes=[
            pltpu.VMEM((2, 1024, 128), BF16),
            pltpu.VMEM((2, 1024, 128), BF16),
            pltpu.VMEM((1024, 256), BF16),
        ],
        compiler_params=params(28),
        name="attend",
    )(place, *shards, laid, laid_bias, cosine, sine)

    got = [parts[0]] + [from_seq(parts[(4 - d) % 4], d) for d in (1, 2, 3)]
    got_other = [swap(v) for v in got]

    others = [swap(after(v, parts[0])) for v in columns]
    out_laid = pl.pallas_call(
        out_lay_kernel,
        out_shape=jax.ShapeDtypeStruct((32, 40, D), BF16),
        in_specs=[SM] + [VM] * 8,
        out_specs=VM,
        compiler_params=params(12),
        name="lay_out",
    )(place, *columns, *others).reshape(8, OWN, D)

    return pl.pallas_call(
        out_kernel,
        out_shape=rows,
        in_specs=[SM] + [VM] * 11,
        out_specs=VM,
        compiler_params=params(12),
        name="project",
    )(place, *got, *got_other, out_laid, embedded, out_bias)


def solution(mesh):
    in_specs = (
        P(("dp", "seq"), None),
        P(),
        P(),
        P(),
        P("dp", None),
        P(),
        P("dp", None),
        P(),
        P("dp", None),
        P("dp", None),
    )
    out_specs = P(("dp", "seq"), None)
    return jax.shard_map(
        per_device, mesh=mesh, in_specs=in_specs, out_specs=out_specs, check_vma=False
    )
```

```python
import functools

import jax
import jax.numpy as jnp
import numpy as np
from jax import lax
from jax.experimental import pallas as pl
from jax.experimental.pallas import tpu as pltpu
from jax.sharding import PartitionSpec as P

HEADS = 16
HDIM = 80
D = 1280
OWN = 2 * HDIM
WIDE = 768
BF16, F32 = jnp.bfloat16, jnp.float32

VM = pl.BlockSpec(memory_space=pltpu.VMEM)
SM = pl.BlockSpec(memory_space=pltpu.SMEM)
BLK = pl.BlockSpec()


def params(mib):
    return pltpu.CompilerParams(vmem_limit_bytes=mib * 1024 * 1024)


def weight(us):
    return pl.CostEstimate(flops=us * 10**9, bytes_accessed=0, transcendentals=0)


def after(value, *earlier):
    return lax.optimization_barrier((value, *earlier))[0]


def seq_shift(dy):
    return [((i + 2 * dy) % 8, i) for i in range(8)]


SWAP = [(i, i ^ 1) for i in range(8)]


def dp_shift(dx, dz):
    return [
        (((x + dx) % 4) * 8 + (z + dz) % 8, x * 8 + z) for x in range(4) for z in range(8)
    ]


X_GROUPS = [[x * 8 + z for x in range(4)] for z in range(8)]


Z_GROUPS = [[x * 8 + z for z in range(8)] for x in range(4)]


def for_each(value, groups):
    return jnp.broadcast_to(value[None], (len(groups[0]), *value.shape))


def exchange(value, groups):
    return lax.all_to_all(value, "dp", 0, 0, tiled=True, axis_index_groups=groups)


def from_seq(value, dy):
    return lax.ppermute(value, "seq", seq_shift(dy))


def swap(value):
    return lax.ppermute(value, "seq", SWAP)


def from_dp(value, dx, dz):
    return lax.ppermute(value, "dp", dp_shift(dx, dz))


def embed_kernel(px, pw, gain, bias, emb_out, norm_out):
    emb = jnp.dot(px[...], pw[...], preferred_element_type=F32).astype(BF16)
    emb_out[...] = emb
    v = emb.astype(F32)
    center = v - jnp.mean(v, axis=-1, keepdims=True)
    var = jnp.mean(center * center, axis=-1, keepdims=True)
    scaled = center * lax.rsqrt(var + 1e-06) * gain[...][None]
    norm_out[...] = (scaled + bias[...][None]).astype(BF16)


def stack_kernel(b0, b1, b2, b3, out):
    blocks = [b[...].astype(F32) for b in (b0, b1, b2, b3)]
    out[...] = jnp.concatenate(blocks, axis=0).astype(BF16)


def write_tables(place, inverse, cos_out, sin_out):
    y, c = place[2], place[3]
    o0, o1, o2 = place[4], place[5], place[6]
    lane = lax.broadcasted_iota(jnp.int32, (128, 128), 1)
    sub = lax.broadcasted_iota(jnp.int32, (128, 128), 0)
    low = jnp.bitwise_and(lane, 63)
    angle = jnp.bitwise_and(sub, 63).astype(F32) * inverse[...]
    mine = (low < HDIM // 4) == (sub < 64)
    both = jnp.concatenate(
        [
            jnp.where(mine, jnp.cos(angle), 0.0),
            jnp.where(mine, jnp.sin(angle) * jnp.where(lane < 64, -1.0, 1.0), 0.0),
        ],
        axis=1,
    )
    parts = []
    for _ in range(3):
        parts.append(both.astype(BF16))
        both = both - parts[-1].astype(F32)
    for r in range(8):
        first = (lax.rem(y + r // 2, 4) * 2 + jnp.bitwise_xor(c, r % 2)) * 128
        pos = first + sub
        second, third = pos >= o1, pos >= o2
        start = jnp.where(third, o2, jnp.where(second, o1, o0))
        across = jnp.where(third, place[9], jnp.where(second, place[8], place[7]))
        within = pos - start
        row = ((within.astype(F32) + 0.5) / across.astype(F32)).astype(jnp.int32)
        column = within - row * across
        pick = (jnp.where(lane < 64, row, column + 64) == lane).astype(F32).astype(BF16)
        total = sum(jnp.dot(pick, part, preferred_element_type=F32) for part in parts)
        cos_out[r] = total[:, :128]
        sin_out[r] = total[:, 128:]


def lay_kernel(place, inverse, *refs):
    blocks, (out, cos_out, sin_out) = refs[:8], refs[8:]
    col = lax.broadcasted_iota(jnp.int32, (3 * OWN, WIDE), 0)
    lane = lax.broadcasted_iota(jnp.int32, (3 * OWN, WIDE), 1)
    piece = sum((col >= HDIM * k).astype(jnp.int32) for k in range(1, 5))
    high = ((col - HDIM * piece >= HDIM // 2) & (col < 4 * HDIM)).astype(jnp.int32)
    pick = (lane == col + 48 * piece + 24 * high).astype(F32).astype(BF16)
    x, z = place[0], place[1]
    for dz in range(8):
        wide = jnp.dot(blocks[dz][...], pick, preferred_element_type=F32).astype(BF16)
        for dx in range(4):
            at = lax.rem(x + dx, 4) * 8 + lax.rem(z + dz, 8)
            out[at] = wide[dx * 40 : dx * 40 + 40]
    write_tables(place, inverse, cos_out, sin_out)


def attend_kernel(place, *refs):
    shards = refs[:8]
    w, b, cosine, sine = refs[8:12]
    outs = refs[12:16]
    qs, ks, vs = refs[16:19]
    scale = float(HDIM**-0.5 * np.log2(np.e))
    y, c, o1, o2 = place[2], place[3], place[5], place[6]

    def first_of(r):
        return (lax.rem(y + r // 2, 4) * 2 + jnp.bitwise_xor(c, r % 2)) * 128

    def image(p):
        return (p >= o1).astype(jnp.int32) + (p >= o2).astype(jnp.int32)

    for blk in range(4):
        rows = pl.ds(blk * 256, 256)
        x = jnp.concatenate([shards[2 * blk][...], shards[2 * blk + 1][...]], axis=0)
        proj = jnp.dot(x, w[...], preferred_element_type=F32) + b[...][None]
        cs = cosine[2 * blk : 2 * blk + 2].reshape(256, 128)
        sn = sine[2 * blk : 2 * blk + 2].reshape(256, 128)
        for h in range(2):
            for first, dst in ((0, qs), (256, ks)):
                t = proj[:, first + h * 128 : first + h * 128 + 128]
                dst[h, rows, :] = (t * cs + pltpu.roll(t, 64, 1) * sn).astype(BF16)
        vs[rows, :] = proj[:, 512:].astype(BF16)
    lane = lax.broadcasted_iota(jnp.int32, (1, 128), 1)
    key_image = jnp.concatenate([image(lane + first_of(r)) for r in range(8)], axis=1)
    row = lax.broadcasted_iota(jnp.int32, (128, 1), 0)
    wide_lane = lax.broadcasted_iota(jnp.int32, (256, 256), 1)
    for blk in range(4):
        rows = pl.ds(blk * 256, 256)
        query_image = jnp.concatenate(
            [image(row + first_of(2 * blk)), image(row + first_of(2 * blk + 1))], axis=0
        )
        allowed = query_image == key_image
        done = []
        for h in range(2):
            s = lax.dot_general(
                qs[h, rows, :], ks[h], (((1,), (1,)), ((), ())), preferred_element_type=F32
            )
            s = jnp.where(allowed, s, -1e30)
            m = jnp.max(s, axis=1, keepdims=True)
            p = jnp.exp2((s - m) * scale).astype(BF16)
            o = jnp.dot(p, vs[...], preferred_element_type=F32)
            done.append(o / o[:, OWN : OWN + 1])
        att = jnp.where(wide_lane < HDIM, done[0], done[1])[:, :OWN]
        outs[blk][...] = jnp.concatenate([att[:128], att[128:]], axis=1).astype(BF16)


def out_kernel(place, *refs):
    here, there = refs[:4], refs[4:8]
    w_own, w_other, emb, bias, out, mixed = refs[8:]
    y, c = place[2], place[3]
    for w, half in ((w_own, c), (w_other, 1 - c)):
        acc = jnp.zeros((128, 640), F32)
        for dy in range(4):
            chip = lax.rem(y + dy, 4) * 2
            acc += jnp.dot(here[dy][:, :OWN], w[chip + c], preferred_element_type=F32)
            acc += jnp.dot(there[dy][:, OWN:], w[chip + 1 - c], preferred_element_type=F32)
        mixed[:, pl.ds(pl.multiple_of(half * 640, 128), 640)] = acc
    out[...] = (emb[...].astype(F32) + mixed[...] + bias[...][None]).astype(BF16)


def halves_apart(piece):
    zero = jnp.zeros(piece.shape[:-1] + (24,), piece.dtype)
    return jnp.concatenate([piece[..., :40], zero, piece[..., 40:], zero], axis=-1)


INVERSE = np.zeros((1, 128), np.float32)
for _l in range(128):
    if _l % 64 < 40:
        INVERSE[0, _l] = 1.0 / 10000.0 ** ((_l % 64 % 20) * 2.0 / 40.0)


def per_device(
    pixels,
    patch_weight,
    ln_gain,
    ln_bias,
    qkv_weight,
    qkv_bias,
    out_weight,
    out_bias,
    offsets,
    widths,
):
    dp, seq = lax.axis_index("dp"), lax.axis_index("seq")
    x, z, y, c = dp // 8, dp % 8, seq // 2, seq % 2
    rows = jax.ShapeDtypeStruct((128, D), BF16)
    place = jnp.concatenate(
        [jnp.stack([x, z, y, c]).astype(jnp.int32), offsets[0], widths[0], jnp.zeros((6,), jnp.int32)]
    )

    blocks = pixels.reshape(32, 4, -1)
    local_pixels = lax.all_to_all(blocks, "dp", 0, 0, tiled=True).reshape(128, -1)

    slices = [lax.dynamic_slice_in_dim(qkv_weight, k * D + seq * OWN, OWN, 1) for k in range(3)]
    mine = after(jnp.concatenate(slices, axis=1), blocks)
    xs = [mine] + [from_dp(mine, d, 0) for d in (1, 2, 3)]
    z0 = pl.pallas_call(
        stack_kernel,
        out_shape=jax.ShapeDtypeStruct((160, 3 * OWN), BF16),
        in_specs=[BLK] * 4,
        out_specs=VM,
        compiler_params=params(4),
        name="stack",
    )(*xs)
    z1, z7 = from_dp(z0, 0, 1), from_dp(z0, 0, 7)
    z2, z6 = from_dp(z1, 0, 1), from_dp(z7, 0, 7)

    embedded, normed = pl.pallas_call(
        embed_kernel,
        out_shape=(rows, rows),
        in_specs=[VM] * 4,
        out_specs=(VM, VM),
        compiler_params=params(12),
        name="embed",
    )(local_pixels, patch_weight, ln_gain, ln_bias)

    same = [normed] + [from_seq(normed, d) for d in (1, 2, 3)]
    crossed = [swap(v) for v in same]
    shards = [v for pair in zip(same, crossed) for v in pair]

    z2, z6 = after(z2, normed), after(z6, normed)
    z3, z5 = from_dp(z2, 0, 1), from_dp(z6, 0, 7)
    z4 = from_dp(z3, 0, 1)
    half = for_each(lax.dynamic_slice_in_dim(out_weight, c * 640, 640, 1), Z_GROUPS)
    column = exchange(after(half, normed, z1, z7), Z_GROUPS)
    column = for_each(column.reshape(320, 640), X_GROUPS)
    o_own = exchange(column, X_GROUPS).reshape(8, OWN, 640)

    laid, cosine, sine = pl.pallas_call(
        lay_kernel,
        out_shape=(
            jax.ShapeDtypeStruct((32, 40, WIDE), BF16),
            jax.ShapeDtypeStruct((8, 128, 128), F32),
            jax.ShapeDtypeStruct((8, 128, 128), F32),
        ),
        in_specs=[SM] + [BLK] * 9,
        out_specs=(VM,) * 3,
        compiler_params=params(12),
        name="lay",
    )(place, jnp.asarray(INVERSE), after(z0, column), z1, z2, z3, z4, z5, z6, z7)
    laid = laid.reshape(D, WIDE)

    own_bias = [lax.dynamic_slice_in_dim(qkv_bias, k * D + seq * OWN, OWN, 0) for k in range(3)]
    ones = jnp.ones((1,), F32)
    laid_bias = jnp.concatenate(
        [halves_apart(own_bias[k][h * HDIM : (h + 1) * HDIM]) for k in range(2) for h in range(2)]
        + [own_bias[2], ones, jnp.zeros((95,), F32)]
    )

    parts = pl.pallas_call(
        attend_kernel,
        out_shape=(jax.ShapeDtypeStruct((128, 2 * OWN), BF16),) * 4,
        in_specs=[SM] + [BLK] * 12,
        out_specs=(VM,) * 4,
        scratch_shapes=[
            pltpu.VMEM((2, 1024, 128), BF16),
            pltpu.VMEM((2, 1024, 128), BF16),
            pltpu.VMEM((1024, 256), BF16),
        ],
        compiler_params=params(18),
        cost_estimate=weight(60),
        name="attend",
    )(place, *shards, laid, laid_bias, cosine, sine)

    got = [parts[0]] + [from_seq(parts[(4 - d) % 4], d) for d in (1, 2, 3)]
    got_other = [swap(v) for v in got]

    o_other = swap(after(o_own, *got[1:]))

    return pl.pallas_call(
        out_kernel,
        out_shape=rows,
        in_specs=[SM] + [BLK] * 12,
        out_specs=VM,
        scratch_shapes=[pltpu.VMEM((128, D), F32)],
        compiler_params=params(12),
        name="project",
    )(place, *got, *got_other, o_own, o_other, embedded, out_bias)


def solution(mesh):
    in_specs = (
        P(("dp", "seq"), None),
        P(),
        P(),
        P(),
        P("dp", None),
        P(),
        P("dp", None),
        P(),
        P("dp", None),
        P("dp", None),
    )
    out_specs = P(("dp", "seq"), None)
    return jax.shard_map(
        per_device, mesh=mesh, in_specs=in_specs, out_specs=out_specs, check_vma=False
    )
```

```python
import functools

import jax
import jax.numpy as jnp
import numpy as np
from jax import lax
from jax.experimental import pallas as pl
from jax.experimental.pallas import tpu as pltpu
from jax.sharding import PartitionSpec as P

HEADS = 16
HDIM = 80
D = 1280
OWN = 2 * HDIM
WIDE = 768
BF16, F32 = jnp.bfloat16, jnp.float32

VM = pl.BlockSpec(memory_space=pltpu.VMEM)
SM = pl.BlockSpec(memory_space=pltpu.SMEM)
BLK = pl.BlockSpec()


def params(mib):
    return pltpu.CompilerParams(vmem_limit_bytes=mib * 1024 * 1024)


def weight(us):
    return pl.CostEstimate(flops=us * 10**9, bytes_accessed=0, transcendentals=0)


def after(value, *earlier):
    return lax.optimization_barrier((value, *earlier))[0]


def seq_shift(dy):
    return [((i + 2 * dy) % 8, i) for i in range(8)]


SWAP = [(i, i ^ 1) for i in range(8)]


def dp_shift(dx, dz):
    return [
        (((x + dx) % 4) * 8 + (z + dz) % 8, x * 8 + z) for x in range(4) for z in range(8)
    ]


X_GROUPS = [[x * 8 + z for x in range(4)] for z in range(8)]


Z_GROUPS = [[x * 8 + z for z in range(8)] for x in range(4)]


def for_each(value, groups):
    return jnp.broadcast_to(value[None], (len(groups[0]), *value.shape))


def exchange(value, groups):
    return lax.all_to_all(value, "dp", 0, 0, tiled=True, axis_index_groups=groups)


def from_seq(value, dy):
    return lax.ppermute(value, "seq", seq_shift(dy))


def swap(value):
    return lax.ppermute(value, "seq", SWAP)


def from_dp(value, dx, dz):
    return lax.ppermute(value, "dp", dp_shift(dx, dz))


def embed_kernel(px, pw, gain, bias, emb_out, norm_out):
    emb = jnp.dot(px[...].reshape(128, 1176), pw[...], preferred_element_type=F32).astype(BF16)
    emb_out[...] = emb
    v = emb.astype(F32)
    center = v - jnp.mean(v, axis=-1, keepdims=True)
    var = jnp.mean(center * center, axis=-1, keepdims=True)
    scaled = center * lax.rsqrt(var + 1e-06) * gain[...][None]
    norm_out[...] = (scaled + bias[...][None]).astype(BF16)


def stack_kernel(b0, b1, b2, b3, half, out, half_out):
    blocks = [b[...].astype(F32) for b in (b0, b1, b2, b3)]
    out[...] = jnp.concatenate(blocks, axis=0).astype(BF16)
    for k in range(8):
        half_out[k] = half[...]


def write_tables(place, inverse, cos_out, sin_out):
    y, c = place[2], place[3]
    o0, o1, o2 = place[4], place[5], place[6]
    lane = lax.broadcasted_iota(jnp.int32, (128, 128), 1)
    sub = lax.broadcasted_iota(jnp.int32, (128, 128), 0)
    low = jnp.bitwise_and(lane, 63)
    angle = jnp.bitwise_and(sub, 63).astype(F32) * inverse[...]
    mine = (low < HDIM // 4) == (sub < 64)
    both = jnp.concatenate(
        [
            jnp.where(mine, jnp.cos(angle), 0.0),
            jnp.where(mine, jnp.sin(angle) * jnp.where(lane < 64, -1.0, 1.0), 0.0),
        ],
        axis=1,
    )
    parts = []
    for _ in range(3):
        parts.append(both.astype(BF16))
        both = both - parts[-1].astype(F32)
    picks = []
    for r in range(8):
        first = (lax.rem(y + r // 2, 4) * 2 + jnp.bitwise_xor(c, r % 2)) * 128
        pos = first + sub
        second, third = pos >= o1, pos >= o2
        start = jnp.where(third, o2, jnp.where(second, o1, o0))
        across = jnp.where(third, place[9], jnp.where(second, place[8], place[7]))
        within = pos - start
        row = ((within.astype(F32) + 0.5) / across.astype(F32)).astype(jnp.int32)
        column = within - row * across
        picks.append((jnp.where(lane < 64, row, column + 64) == lane).astype(F32).astype(BF16))
    pick = jnp.concatenate(picks, axis=0)
    total = sum(jnp.dot(pick, part, preferred_element_type=F32) for part in parts)
    for r in range(8):
        cos_out[r] = total[r * 128 : r * 128 + 128, :128]
        sin_out[r] = total[r * 128 : r * 128 + 128, 128:]


def lay_kernel(place, inverse, *refs):
    blocks, (out, cos_out, sin_out) = refs[:8], refs[8:]
    col = lax.broadcasted_iota(jnp.int32, (3 * OWN, WIDE), 0)
    lane = lax.broadcasted_iota(jnp.int32, (3 * OWN, WIDE), 1)
    piece = sum((col >= HDIM * k).astype(jnp.int32) for k in range(1, 5))
    high = ((col - HDIM * piece >= HDIM // 2) & (col < 4 * HDIM)).astype(jnp.int32)
    pick = (lane == col + 48 * piece + 24 * high).astype(F32).astype(BF16)
    x, z = place[0], place[1]
    rows = jnp.concatenate([block[...] for block in blocks], axis=0)
    wide = jnp.dot(rows, pick, preferred_element_type=F32)
    for dz in range(8):
        for dx in range(4):
            at = lax.rem(x + dx, 4) * 8 + lax.rem(z + dz, 8)
            first = dz * 160 + dx * 40
            out[at] = wide[first : first + 40].astype(BF16)
    write_tables(place, inverse, cos_out, sin_out)


def attend_kernel(place, *refs):
    shards = refs[:8]
    w, b, cosine, sine = refs[8:12]
    outs = refs[12:16]
    qs, ks, vs = refs[16:19]
    scale = float(HDIM**-0.5 * np.log2(np.e))
    y, c, o1, o2 = place[2], place[3], place[5], place[6]

    def first_of(r):
        return (lax.rem(y + r // 2, 4) * 2 + jnp.bitwise_xor(c, r % 2)) * 128

    def image(p):
        return (p >= o1).astype(jnp.int32) + (p >= o2).astype(jnp.int32)

    for blk in range(4):
        rows = pl.ds(blk * 256, 256)
        x = jnp.concatenate([shards[2 * blk][...], shards[2 * blk + 1][...]], axis=0)
        proj = jnp.dot(x, w[...], preferred_element_type=F32) + b[...][None]
        cs = cosine[2 * blk : 2 * blk + 2].reshape(256, 128)
        sn = sine[2 * blk : 2 * blk + 2].reshape(256, 128)
        for h in range(2):
            for first, dst in ((0, qs), (256, ks)):
                t = proj[:, first + h * 128 : first + h * 128 + 128]
                dst[h, rows, :] = (t * cs + pltpu.roll(t, 64, 1) * sn).astype(BF16)
        vs[rows, :] = proj[:, 512:].astype(BF16)
    lane = lax.broadcasted_iota(jnp.int32, (1, 128), 1)
    key_image = jnp.concatenate([image(lane + first_of(r)) for r in range(8)], axis=1)
    row = lax.broadcasted_iota(jnp.int32, (128, 1), 0)
    wide_lane = lax.broadcasted_iota(jnp.int32, (256, 256), 1)
    for blk in range(4):
        rows = pl.ds(blk * 256, 256)
        query_image = jnp.concatenate(
            [image(row + first_of(2 * blk)), image(row + first_of(2 * blk + 1))], axis=0
        )
        allowed = query_image == key_image
        done = []
        for h in range(2):
            s = lax.dot_general(
                qs[h, rows, :], ks[h], (((1,), (1,)), ((), ())), preferred_element_type=F32
            )
            s = jnp.where(allowed, s, -1e30)
            m = jnp.max(s, axis=1, keepdims=True)
            p = jnp.exp2((s - m) * scale).astype(BF16)
            o = jnp.dot(p, vs[...], preferred_element_type=F32)
            done.append(o / o[:, OWN : OWN + 1])
        att = jnp.where(wide_lane < HDIM, done[0], done[1])[:, :OWN]
        outs[blk][...] = jnp.concatenate([att[:128], att[128:]], axis=1).astype(BF16)


def out_kernel(place, *refs):
    here, there = refs[:4], refs[4:8]
    w_own, w_other, emb, bias, out, mixed = refs[8:]
    y, c = place[2], place[3]
    for w, half in ((w_own, c), (w_other, 1 - c)):
        acc = jnp.zeros((128, 640), F32)
        for dy in range(4):
            chip = lax.rem(y + dy, 4) * 2
            acc += jnp.dot(here[dy][:, :OWN], w[chip + c], preferred_element_type=F32)
            acc += jnp.dot(there[dy][:, OWN:], w[chip + 1 - c], preferred_element_type=F32)
        mixed[:, pl.ds(pl.multiple_of(half * 640, 128), 640)] = acc
    out[...] = (emb[...].astype(F32) + mixed[...] + bias[...][None]).astype(BF16)


def halves_apart(piece):
    zero = jnp.zeros(piece.shape[:-1] + (24,), piece.dtype)
    return jnp.concatenate([piece[..., :40], zero, piece[..., 40:], zero], axis=-1)


INVERSE = np.zeros((1, 128), np.float32)
for _l in range(128):
    if _l % 64 < 40:
        INVERSE[0, _l] = 1.0 / 10000.0 ** ((_l % 64 % 20) * 2.0 / 40.0)


def per_device(
    pixels,
    patch_weight,
    ln_gain,
    ln_bias,
    qkv_weight,
    qkv_bias,
    out_weight,
    out_bias,
    offsets,
    widths,
):
    dp, seq = lax.axis_index("dp"), lax.axis_index("seq")
    x, z, y, c = dp // 8, dp % 8, seq // 2, seq % 2
    rows = jax.ShapeDtypeStruct((128, D), BF16)
    place = jnp.concatenate(
        [jnp.stack([x, z, y, c]).astype(jnp.int32), offsets[0], widths[0], jnp.zeros((6,), jnp.int32)]
    )

    blocks = pixels.reshape(32, 4, -1)
    local_pixels = lax.all_to_all(blocks, "dp", 0, 0, tiled=True)

    slices = [lax.dynamic_slice_in_dim(qkv_weight, k * D + seq * OWN, OWN, 1) for k in range(3)]
    mine = after(jnp.concatenate(slices, axis=1), blocks)
    xs = [mine] + [from_dp(mine, d, 0) for d in (1, 2, 3)]
    half = lax.dynamic_slice_in_dim(out_weight, c * 640, 640, 1)
    z0, half = pl.pallas_call(
        stack_kernel,
        out_shape=(
            jax.ShapeDtypeStruct((160, 3 * OWN), BF16),
            jax.ShapeDtypeStruct((8, 40, 640), BF16),
        ),
        in_specs=[BLK] * 5,
        out_specs=(VM,) * 2,
        compiler_params=params(4),
        name="stack",
    )(*xs, half)
    z1, z7 = from_dp(z0, 0, 1), from_dp(z0, 0, 7)
    z2, z6 = from_dp(z1, 0, 1), from_dp(z7, 0, 7)

    embedded, normed = pl.pallas_call(
        embed_kernel,
        out_shape=(rows, rows),
        in_specs=[VM] * 4,
        out_specs=(VM, VM),
        compiler_params=params(12),
        name="embed",
    )(local_pixels, patch_weight, ln_gain, ln_bias)

    same = [normed] + [from_seq(normed, d) for d in (1, 2, 3)]
    crossed = [swap(v) for v in same]
    shards = [v for pair in zip(same, crossed) for v in pair]

    z2, z6 = after(z2, normed), after(z6, normed)
    z3, z5 = from_dp(z2, 0, 1), from_dp(z6, 0, 7)
    z4 = from_dp(z3, 0, 1)
    column = exchange(after(half, normed, z1, z7), Z_GROUPS)
    column = for_each(column.reshape(320, 640), X_GROUPS)
    o_own = exchange(column, X_GROUPS).reshape(8, OWN, 640)

    laid, cosine, sine = pl.pallas_call(
        lay_kernel,
        out_shape=(
            jax.ShapeDtypeStruct((32, 40, WIDE), BF16),
            jax.ShapeDtypeStruct((8, 128, 128), F32),
            jax.ShapeDtypeStruct((8, 128, 128), F32),
        ),
        in_specs=[SM] + [BLK] * 9,
        out_specs=(VM,) * 3,
        compiler_params=params(12),
        name="lay",
    )(place, jnp.asarray(INVERSE), after(z0, column), z1, z2, z3, z4, z5, z6, z7)
    laid = laid.reshape(D, WIDE)

    own_bias = [lax.dynamic_slice_in_dim(qkv_bias, k * D + seq * OWN, OWN, 0) for k in range(3)]
    ones = jnp.ones((1,), F32)
    laid_bias = jnp.concatenate(
        [halves_apart(own_bias[k][h * HDIM : (h + 1) * HDIM]) for k in range(2) for h in range(2)]
        + [own_bias[2], ones, jnp.zeros((95,), F32)]
    )

    parts = pl.pallas_call(
        attend_kernel,
        out_shape=(jax.ShapeDtypeStruct((128, 2 * OWN), BF16),) * 4,
        in_specs=[SM] + [BLK] * 12,
        out_specs=(VM,) * 4,
        scratch_shapes=[
            pltpu.VMEM((2, 1024, 128), BF16),
            pltpu.VMEM((2, 1024, 128), BF16),
            pltpu.VMEM((1024, 256), BF16),
        ],
        compiler_params=params(18),
        cost_estimate=weight(60),
        name="attend",
    )(place, *shards, laid, laid_bias, cosine, sine)

    got = [parts[0]] + [from_seq(parts[(4 - d) % 4], d) for d in (1, 2, 3)]
    got_other = [swap(v) for v in got]

    o_other = swap(after(o_own, *got[1:]))

    return pl.pallas_call(
        out_kernel,
        out_shape=rows,
        in_specs=[SM] + [BLK] * 12,
        out_specs=VM,
        scratch_shapes=[pltpu.VMEM((128, D), F32)],
        compiler_params=params(12),
        name="project",
    )(place, *got, *got_other, o_own, o_other, embedded, out_bias)


def solution(mesh):
    in_specs = (
        P(("dp", "seq"), None),
        P(),
        P(),
        P(),
        P("dp", None),
        P(),
        P("dp", None),
        P(),
        P("dp", None),
        P("dp", None),
    )
    out_specs = P(("dp", "seq"), None)
    return jax.shard_map(
        per_device, mesh=mesh, in_specs=in_specs, out_specs=out_specs, check_vma=False
    )
```

```python
import functools

import jax
import jax.numpy as jnp
import numpy as np
from jax import lax
from jax.experimental import pallas as pl
from jax.experimental.pallas import tpu as pltpu
from jax.sharding import PartitionSpec as P

HEADS = 16
HDIM = 80
D = 1280
OWN = 2 * HDIM
WIDE = 768
BF16, F32 = jnp.bfloat16, jnp.float32

VM = pl.BlockSpec(memory_space=pltpu.VMEM)
SM = pl.BlockSpec(memory_space=pltpu.SMEM)
BLK = pl.BlockSpec()


def params(mib):
    return pltpu.CompilerParams(vmem_limit_bytes=mib * 1024 * 1024)


def weight(us):
    return pl.CostEstimate(flops=us * 10**9, bytes_accessed=0, transcendentals=0)


def after(value, *earlier):
    return lax.optimization_barrier((value, *earlier))[0]


def seq_shift(dy):
    return [((i + 2 * dy) % 8, i) for i in range(8)]


SWAP = [(i, i ^ 1) for i in range(8)]


def dp_shift(dx, dz):
    return [
        (((x + dx) % 4) * 8 + (z + dz) % 8, x * 8 + z) for x in range(4) for z in range(8)
    ]


X_GROUPS = [[x * 8 + z for x in range(4)] for z in range(8)]


Z_GROUPS = [[x * 8 + z for z in range(8)] for x in range(4)]


def for_each(value, groups):
    return jnp.broadcast_to(value[None], (len(groups[0]), *value.shape))


def exchange(value, groups):
    return lax.all_to_all(value, "dp", 0, 0, tiled=True, axis_index_groups=groups)


def from_seq(value, dy):
    return lax.ppermute(value, "seq", seq_shift(dy))


def swap(value):
    return lax.ppermute(value, "seq", SWAP)


def from_dp(value, dx, dz):
    return lax.ppermute(value, "dp", dp_shift(dx, dz))


def embed_kernel(px, pw, gain, bias, emb_out, norm_out):
    emb = jnp.dot(px[...].reshape(128, 1176), pw[...], preferred_element_type=F32).astype(BF16)
    emb_out[...] = emb
    v = emb.astype(F32)
    center = v - jnp.mean(v, axis=-1, keepdims=True)
    var = jnp.mean(center * center, axis=-1, keepdims=True)
    scaled = center * lax.rsqrt(var + 1e-06) * gain[...][None]
    norm_out[...] = (scaled + bias[...][None]).astype(BF16)


def stack_kernel(b0, b1, b2, b3, half, out, half_out):
    blocks = [b[...].astype(F32) for b in (b0, b1, b2, b3)]
    out[...] = jnp.concatenate(blocks, axis=0).astype(BF16)
    for k in range(8):
        half_out[k] = half[...]


def write_tables(place, inverse, cos_out, sin_out):
    y, c = place[2], place[3]
    o0, o1, o2 = place[4], place[5], place[6]
    lane = lax.broadcasted_iota(jnp.int32, (128, 128), 1)
    sub = lax.broadcasted_iota(jnp.int32, (128, 128), 0)
    low = jnp.bitwise_and(lane, 63)
    angle = jnp.bitwise_and(sub, 63).astype(F32) * inverse[...]
    mine = (low < HDIM // 4) == (sub < 64)
    both = jnp.concatenate(
        [
            jnp.where(mine, jnp.cos(angle), 0.0),
            jnp.where(mine, jnp.sin(angle) * jnp.where(lane < 64, -1.0, 1.0), 0.0),
        ],
        axis=1,
    )
    parts = []
    for _ in range(3):
        parts.append(both.astype(BF16))
        both = both - parts[-1].astype(F32)
    picks = []
    for r in range(8):
        first = (lax.rem(y + r // 2, 4) * 2 + jnp.bitwise_xor(c, r % 2)) * 128
        pos = first + sub
        second, third = pos >= o1, pos >= o2
        start = jnp.where(third, o2, jnp.where(second, o1, o0))
        across = jnp.where(third, place[9], jnp.where(second, place[8], place[7]))
        within = pos - start
        row = ((within.astype(F32) + 0.5) / across.astype(F32)).astype(jnp.int32)
        column = within - row * across
        picks.append((jnp.where(lane < 64, row, column + 64) == lane).astype(F32).astype(BF16))
    pick = jnp.concatenate(picks, axis=0)
    total = sum(jnp.dot(pick, part, preferred_element_type=F32) for part in parts)
    for r in range(8):
        cos_out[r] = total[r * 128 : r * 128 + 128, :128]
        sin_out[r] = total[r * 128 : r * 128 + 128, 128:]


def lay_kernel(place, inverse, *refs):
    blocks, (out, cos_out, sin_out) = refs[:8], refs[8:]
    col = lax.broadcasted_iota(jnp.int32, (3 * OWN, WIDE), 0)
    lane = lax.broadcasted_iota(jnp.int32, (3 * OWN, WIDE), 1)
    piece = sum((col >= HDIM * k).astype(jnp.int32) for k in range(1, 5))
    high = ((col - HDIM * piece >= HDIM // 2) & (col < 4 * HDIM)).astype(jnp.int32)
    pick = (lane == col + 48 * piece + 24 * high).astype(F32).astype(BF16)
    x, z = place[0], place[1]
    rows = jnp.concatenate([block[...] for block in blocks], axis=0)
    wide = jnp.dot(rows, pick, preferred_element_type=F32)
    for dz in range(8):
        for dx in range(4):
            at = lax.rem(x + dx, 4) * 8 + lax.rem(z + dz, 8)
            first = dz * 160 + dx * 40
            out[at] = wide[first : first + 40].astype(BF16)
    write_tables(place, inverse, cos_out, sin_out)


def attend_kernel(place, *refs):
    shards = refs[:8]
    w, b, cosine, sine = refs[8:12]
    outs = refs[12:16]
    qs, ks, vs = refs[16:19]
    scale = float(HDIM**-0.5 * np.log2(np.e))
    y, c, o1, o2 = place[2], place[3], place[5], place[6]

    def first_of(r):
        return (lax.rem(y + r // 2, 4) * 2 + jnp.bitwise_xor(c, r % 2)) * 128

    def image(p):
        return (p >= o1).astype(jnp.int32) + (p >= o2).astype(jnp.int32)

    for blk in range(4):
        rows = pl.ds(blk * 256, 256)
        x = jnp.concatenate([shards[2 * blk][...], shards[2 * blk + 1][...]], axis=0)
        proj = jnp.dot(x, w[...], preferred_element_type=F32) + b[...][None]
        cs = cosine[2 * blk : 2 * blk + 2].reshape(256, 128)
        sn = sine[2 * blk : 2 * blk + 2].reshape(256, 128)
        for h in range(2):
            for first, dst in ((0, qs), (256, ks)):
                t = proj[:, first + h * 128 : first + h * 128 + 128]
                dst[h, rows, :] = (t * cs + pltpu.roll(t, 64, 1) * sn).astype(BF16)
        vs[rows, :] = proj[:, 512:].astype(BF16)
    lane = lax.broadcasted_iota(jnp.int32, (1, 128), 1)
    key_image = jnp.concatenate([image(lane + first_of(r)) for r in range(8)], axis=1)
    row = lax.broadcasted_iota(jnp.int32, (128, 1), 0)
    wide_lane = lax.broadcasted_iota(jnp.int32, (256, 256), 1)
    for blk in range(4):
        rows = pl.ds(blk * 256, 256)
        query_image = jnp.concatenate(
            [image(row + first_of(2 * blk)), image(row + first_of(2 * blk + 1))], axis=0
        )
        allowed = query_image == key_image
        done = []
        for h in range(2):
            s = lax.dot_general(
                qs[h, rows, :], ks[h], (((1,), (1,)), ((), ())), preferred_element_type=F32
            )
            s = jnp.where(allowed, s, -1e30)
            m = jnp.max(s, axis=1, keepdims=True)
            p = jnp.exp2((s - m) * scale).astype(BF16)
            o = jnp.dot(p, vs[...], preferred_element_type=F32)
            done.append(o / o[:, OWN : OWN + 1])
        att = jnp.where(wide_lane < HDIM, done[0], done[1])[:, :OWN]
        outs[blk][...] = jnp.concatenate([att[:128], att[128:]], axis=1).astype(BF16)


def out_kernel(place, *refs):
    here, there = refs[:4], refs[4:8]
    w_own, w_other, emb, bias, out, mixed = refs[8:]
    y, c = place[2], place[3]
    for w, half in ((w_own, c), (w_other, 1 - c)):
        acc = jnp.zeros((128, 640), F32)
        for dy in range(4):
            chip = lax.rem(y + dy, 4) * 2
            acc += jnp.dot(here[dy][:, :OWN], w[chip + c], preferred_element_type=F32)
            acc += jnp.dot(there[dy][:, OWN:], w[chip + 1 - c], preferred_element_type=F32)
        mixed[:, pl.ds(pl.multiple_of(half * 640, 128), 640)] = acc
    out[...] = (emb[...].astype(F32) + mixed[...] + bias[...][None]).astype(BF16)


def halves_apart(piece):
    zero = jnp.zeros(piece.shape[:-1] + (24,), piece.dtype)
    return jnp.concatenate([piece[..., :40], zero, piece[..., 40:], zero], axis=-1)


INVERSE = np.zeros((1, 128), np.float32)
for _l in range(128):
    if _l % 64 < 40:
        INVERSE[0, _l] = 1.0 / 10000.0 ** ((_l % 64 % 20) * 2.0 / 40.0)


def per_device(
    pixels,
    patch_weight,
    ln_gain,
    ln_bias,
    qkv_weight,
    qkv_bias,
    out_weight,
    out_bias,
    offsets,
    widths,
):
    dp, seq = lax.axis_index("dp"), lax.axis_index("seq")
    x, z, y, c = dp // 8, dp % 8, seq // 2, seq % 2
    rows = jax.ShapeDtypeStruct((128, D), BF16)
    place = jnp.concatenate(
        [jnp.stack([x, z, y, c]).astype(jnp.int32), offsets[0], widths[0], jnp.zeros((6,), jnp.int32)]
    )

    blocks = pixels.reshape(32, 4, -1)
    local_pixels = lax.all_to_all(blocks, "dp", 0, 0, tiled=True)

    slices = [lax.dynamic_slice_in_dim(qkv_weight, k * D + seq * OWN, OWN, 1) for k in range(3)]
    mine = after(jnp.concatenate(slices, axis=1), blocks)
    xs = [mine] + [from_dp(mine, d, 0) for d in (1, 2, 3)]
    half = lax.dynamic_slice_in_dim(out_weight, c * 640, 640, 1)
    z0, half = pl.pallas_call(
        stack_kernel,
        out_shape=(
            jax.ShapeDtypeStruct((160, 3 * OWN), BF16),
            jax.ShapeDtypeStruct((8, 40, 640), BF16),
        ),
        in_specs=[BLK] * 5,
        out_specs=(VM,) * 2,
        compiler_params=params(4),
        name="stack",
    )(*xs, half)
    z1, z7 = from_dp(z0, 0, 1), from_dp(z0, 0, 7)
    z2, z6 = from_dp(z1, 0, 1), from_dp(z7, 0, 7)

    embedded, normed = pl.pallas_call(
        embed_kernel,
        out_shape=(rows, rows),
        in_specs=[VM] * 4,
        out_specs=(VM, VM),
        compiler_params=params(12),
        name="embed",
    )(local_pixels, patch_weight, ln_gain, ln_bias)

    same = [normed] + [from_seq(normed, d) for d in (1, 2, 3)]
    crossed = [swap(v) for v in same]
    shards = [v for pair in zip(same, crossed) for v in pair]

    z2, z6 = after(z2, normed), after(z6, normed)
    z3, z5 = from_dp(z2, 0, 1), from_dp(z6, 0, 7)
    z4 = from_dp(z3, 0, 1)
    column = exchange(after(half, normed, z1, z7), Z_GROUPS)
    column = for_each(column.reshape(320, 640), X_GROUPS)
    o_own = exchange(column, X_GROUPS).reshape(8, OWN, 640)

    laid, cosine, sine = pl.pallas_call(
        lay_kernel,
        out_shape=(
            jax.ShapeDtypeStruct((32, 40, WIDE), BF16),
            jax.ShapeDtypeStruct((8, 128, 128), F32),
            jax.ShapeDtypeStruct((8, 128, 128), F32),
        ),
        in_specs=[SM] + [BLK] * 9,
        out_specs=(VM,) * 3,
        compiler_params=params(12),
        name="lay",
    )(place, jnp.asarray(INVERSE), after(z0, column), z1, z2, z3, z4, z5, z6, z7)
    laid = laid.reshape(D, WIDE)

    own_bias = [lax.dynamic_slice_in_dim(qkv_bias, k * D + seq * OWN, OWN, 0) for k in range(3)]
    ones = jnp.ones((1,), F32)
    laid_bias = jnp.concatenate(
        [halves_apart(own_bias[k][h * HDIM : (h + 1) * HDIM]) for k in range(2) for h in range(2)]
        + [own_bias[2], ones, jnp.zeros((95,), F32)]
    )

    parts = pl.pallas_call(
        attend_kernel,
        out_shape=(jax.ShapeDtypeStruct((128, 2 * OWN), BF16),) * 4,
        in_specs=[SM] + [BLK] * 12,
        out_specs=(VM,) * 4,
        scratch_shapes=[
            pltpu.VMEM((2, 1024, 128), BF16),
            pltpu.VMEM((2, 1024, 128), BF16),
            pltpu.VMEM((1024, 256), BF16),
        ],
        compiler_params=params(18),
        cost_estimate=weight(60),
        name="attend",
    )(place, *shards, laid, laid_bias, cosine, sine)

    got = [parts[0]] + [from_seq(parts[(4 - d) % 4], d) for d in (1, 2, 3)]
    got_other = [swap(v) for v in got]

    o_other = swap(after(o_own, got[1], got[3]))

    return pl.pallas_call(
        out_kernel,
        out_shape=rows,
        in_specs=[SM] + [BLK] * 12,
        out_specs=VM,
        scratch_shapes=[pltpu.VMEM((128, D), F32)],
        compiler_params=params(12),
        name="project",
    )(place, *got, *got_other, o_own, o_other, embedded, out_bias)


def solution(mesh):
    in_specs = (
        P(("dp", "seq"), None),
        P(),
        P(),
        P(),
        P("dp", None),
        P(),
        P("dp", None),
        P(),
        P("dp", None),
        P("dp", None),
    )
    out_specs = P(("dp", "seq"), None)
    return jax.shard_map(
        per_device, mesh=mesh, in_specs=in_specs, out_specs=out_specs, check_vma=False
    )
```
